32 devices in a mesh: wide: 4 (over z), narrow: 8 (over y, x, core).
Axes of the slice: x: 2, y: 2, z: 4, core: 2. Of those that a mesh axis runs over, the one named last changes fastest.
Arguments:
- hidden: bfloat16 [512, 4096], P('wide', 'narrow'), may hold values from -6 to 6
- norm_gain: float32 [4096], replicated, may hold values from 0.1 to 1.9
- w_query: bfloat16 [4096, 8192], P(None, 'narrow'), may hold values from -0.09375 to 0.09375
- w_keyval: bfloat16 [4096, 1024], P('narrow'), may hold values from -0.09375 to 0.09375
- query_gain: float32 [128], replicated, may hold values from 0.5 to 4
- key_gain: float32 [128], replicated, may hold values from 0.5 to 4
- cache_keys: bfloat16 [32, 16384, 512], P('wide', 'narrow'), may hold values from -300 to 300
- cache_values: bfloat16 [32, 16384, 512], P('wide', 'narrow'), may hold values from -6 to 6
- cache_lengths: int32 [32], P('wide'), may hold values from 1 to 16384
- owner_rank: int32 [32], P('wide'), may hold values from 0 to 3, as said below
- draft_mask: int32 [32, 16, 16], P('wide'), may hold values from 0 to 1, as said below
- w_output: bfloat16 [8192, 4096], P('narrow'), may hold values from -0.0625 to 0.0625
Outputs:
- projected: bfloat16 [512, 4096], P('wide', 'narrow')
The draws below stay inside these ranges and needn't reach their ends.
Inputs may be any that keep to these rules, and one draw needn't show every extreme that they name: `owner_rank`: in each aligned block of 8 requests every index of wide is named exactly 2 times. Row t of a request marks the ancestors of draft token t in a tree of draft tokens and t itself: draft_mask[r, t, t] = 1 and draft_mask[r, t, u] = 0 for u > t.
All inputs are finite; a program needn't handle non-finite values.
Results may differ from the reference program's by a relative error of at most 0.007.
The reference program's roundings to bfloat16 on the way count: a program that leaves them out, or rounds other values in their place, can miss the bound.
Values may be sent and summed in bfloat16 or wider, within the bound.
A program may use at most 192 MiB of HBM per device.

```python
import math
import jax
import jax.numpy as jnp
from jax import lax

D = 4096
HQ = 64
KVH = 4
HD = 128
DRAFT = 16
WIN = 16384
REQ_DEV = 8
REQS = 32
TOKENS = 512
CAP = 2


def draw_cache_keys(key, part):
    normals = jax.random.normal(jax.random.fold_in(key, 11), (REQS, WIN, KVH * HD), jnp.float32) * 2.0
    return jnp.clip(normals, -300.0, 300.0).astype(jnp.bfloat16)


def draw_owner_rank(key, part):
    sources = REQS // REQ_DEV
    per_pair = REQ_DEV // sources

    def one_source(index):
        return jax.random.permutation(jax.random.fold_in(jax.random.fold_in(key, 21), index), REQ_DEV) // per_pair
    ranks = jax.vmap(one_source)(jnp.arange(sources, dtype=jnp.int32))
    return ranks.reshape(REQS).astype(jnp.int32)


def draw_draft_mask(key, part):

    def one_request(request_key):
        upper = jnp.maximum(jnp.arange(DRAFT, dtype=jnp.int32), 1)
        parents = jax.random.randint(request_key, (DRAFT,), 0, upper)
        identity = jnp.eye(DRAFT, dtype=jnp.int32)
        ancestry = identity
        for index in range(1, DRAFT):
            ancestry = ancestry.at[index].set(jnp.maximum(ancestry[parents[index]], identity[index]))
        return ancestry
    request_keys = jax.random.split(jax.random.fold_in(key, 31), REQS)
    return jax.vmap(one_request)(request_keys).astype(jnp.int32)


def set_ends(array, own_key, least, top_value):
    extent = array.shape
    place = [jax.random.randint(jax.random.fold_in(own_key, axis), (), 0, extent[axis]) for axis in range(len(extent))]
    array = array.at[tuple(place)].set(least)
    longest = extent.index(max(extent))
    place[longest] = (place[longest] + 1) % extent[longest]
    return array.at[tuple(place)].set(top_value)


def level_of(own_key, dims, cuts, low, largest):
    level, own = 1.0, jax.random.fold_in(own_key, 6)
    for position, shards_of in cuts:
        steps = jnp.exp(jax.random.uniform(jax.random.fold_in(own, position), (shards_of,), jnp.float32, low / len(cuts), largest / len(cuts)))
        level = level * jnp.repeat(steps, dims[position] // shards_of).reshape([-1 if axis == position else 1 for axis in range(len(dims))])
    return level


def bell_draw(stream_key, dims, spread, most, cuts=(), held_as=jnp.bfloat16):
    entries = spread * jax.random.normal(stream_key, dims, jnp.float32)
    if cuts:
        entries = entries * level_of(stream_key, dims, cuts, -0.22, 0.18)
    return jnp.clip(entries, -most, most).astype(held_as)


def setup_inputs(seed: int = 0) -> dict:
    key_of = jax.random.split(jax.random.key(seed), 13)
    hidden = bell_draw(key_of[0], (TOKENS, D), 1.0, 6.0, ((0, 4), (1, 8)))
    norm_gain = jnp.clip(1.0 + 0.18 * jax.random.normal(key_of[1], (D,), jnp.float32), 0.1, 1.9)
    w_query = bell_draw(key_of[2], (D, HQ * HD), D ** -0.5, 0.09375, ((1, 8),))
    w_keyval = bell_draw(key_of[3], (D, 2 * KVH * HD), D ** -0.5, 0.09375, ((0, 8),))
    query_gain = jnp.clip(jnp.exp(jax.random.uniform(key_of[4], (HD,), jnp.float32, math.log(0.5), math.log(4.0))), 0.5, 4.0)
    key_gain = jnp.clip(jnp.exp(jax.random.uniform(key_of[5], (HD,), jnp.float32, math.log(0.5), math.log(4.0))), 0.5, 4.0)
    cache_keys = draw_cache_keys(jax.random.fold_in(key_of[12], 71), 0)
    cache_values = bell_draw(key_of[7], (REQS, WIN, KVH * HD), 1.0, 6.0, ((0, 4), (1, 8)))
    cache_lengths = set_ends(jax.random.randint(key_of[8], (REQS,), 1, WIN + 1), jax.random.fold_in(key_of[8], 1), 1, WIN).astype(jnp.int32)
    owner_rank = draw_owner_rank(jax.random.fold_in(key_of[12], 71), 0)
    draft_mask = draw_draft_mask(jax.random.fold_in(key_of[12], 71), 0)
    w_output = bell_draw(key_of[11], (HQ * HD, D), (HQ * HD) ** -0.5, 0.0625, ((0, 8),))
    return {"hidden": hidden, "norm_gain": norm_gain, "w_query": w_query, "w_keyval": w_keyval, "query_gain": query_gain, "key_gain": key_gain, "cache_keys": cache_keys, "cache_values": cache_values, "cache_lengths": cache_lengths, "owner_rank": owner_rank, "draft_mask": draft_mask, "w_output": w_output}


epsilon = 1e-06
masked_fill = -1e+30

def rms_norm(values, gain_row):
    return values * lax.rsqrt(lax.optimization_barrier(jnp.mean(values * values, axis=-1, keepdims=True)) + epsilon) * gain_row

def reference(hidden, norm_gain, w_query, w_keyval, query_gain, key_gain, cache_keys, cache_values, cache_lengths, owner_rank, draft_mask, w_output):
    group = HQ // KVH
    inv_sqrt = 1.0 / math.sqrt(HD)
    normed = rms_norm(hidden.astype(jnp.float32), norm_gain.astype(jnp.float32)).astype(jnp.bfloat16)
    queries = jnp.dot(normed, w_query, preferred_element_type=jnp.float32).reshape(TOKENS, HQ, HD)
    queries = rms_norm(queries, query_gain.astype(jnp.float32)).astype(jnp.bfloat16)
    keyval = jnp.dot(normed, w_keyval, preferred_element_type=jnp.float32)
    new_keys = rms_norm(keyval[:, :KVH * HD].reshape(TOKENS, KVH, HD), key_gain.astype(jnp.float32)).astype(jnp.bfloat16)
    new_values = keyval[:, KVH * HD:].reshape(TOKENS, KVH, HD).astype(jnp.bfloat16)
    request_ids = jnp.arange(REQS, dtype=jnp.int32)
    source = request_ids // REQ_DEV
    earlier_same = (source[:, None] == source[None, :]) & (owner_rank[:, None] == owner_rank[None, :]) & (request_ids[None, :] < request_ids[:, None])
    rank_within = lax.optimization_barrier(jnp.sum(earlier_same.astype(jnp.int32), axis=1)).astype(jnp.int32)
    cache_slot = (owner_rank * REQ_DEV + source * CAP + rank_within).astype(jnp.int32)

    def attend(request_args):
        query_rows, key_rows, value_rows, slot_index, mask_rows = request_args
        cached_k = cache_keys[slot_index].reshape(WIN, KVH, HD).astype(jnp.float32)
        cached_v = cache_values[slot_index].reshape(WIN, KVH, HD).astype(jnp.float32)
        live_length = cache_lengths[slot_index]
        grouped = query_rows.reshape(DRAFT, KVH, group, HD).astype(jnp.float32)
        cache_scores = jnp.einsum('tkgd,skd->kgts', grouped, cached_k) * inv_sqrt
        live_keys = jnp.arange(WIN, dtype=jnp.int32) < live_length
        cache_scores = jnp.where(live_keys, cache_scores, masked_fill)
        draft_scores = jnp.einsum('tkgd,skd->kgts', grouped, key_rows.astype(jnp.float32)) * inv_sqrt
        allowed = mask_rows == 1
        draft_scores = jnp.where(allowed, draft_scores, masked_fill)
        maxima = jnp.maximum(lax.optimization_barrier(jnp.max(cache_scores, axis=-1)), lax.optimization_barrier(jnp.max(draft_scores, axis=-1)))[..., None]
        cache_weights = jnp.where(live_keys, jnp.exp(cache_scores - maxima), 0.0)
        draft_weights = jnp.where(allowed, jnp.exp(draft_scores - maxima), 0.0)
        totals = lax.optimization_barrier(jnp.sum(cache_weights, axis=-1)) + lax.optimization_barrier(jnp.sum(draft_weights, axis=-1))
        weighted = jnp.einsum('kgts,skd->kgtd', cache_weights.astype(jnp.bfloat16).astype(jnp.float32), cached_v)
        weighted = weighted + jnp.einsum('kgts,skd->kgtd', draft_weights.astype(jnp.bfloat16).astype(jnp.float32), value_rows.astype(jnp.float32))
        output = weighted / totals[..., None]
        return output.transpose(2, 0, 1, 3).reshape(DRAFT, HQ * HD).astype(jnp.bfloat16)
    attended = lax.map(attend, (queries.reshape(REQS, DRAFT, HQ, HD), new_keys.reshape(REQS, DRAFT, KVH, HD), new_values.reshape(REQS, DRAFT, KVH, HD), cache_slot, draft_mask))
    attended = attended.reshape(TOKENS, HQ * HD)
    return jnp.dot(attended, w_output, preferred_element_type=jnp.float32).astype(jnp.bfloat16)
```

```python
import functools
import math

import jax
import jax.numpy as jnp
from jax import lax
from jax.experimental import pallas as pl
from jax.experimental.pallas import tpu as pltpu
from jax.sharding import PartitionSpec as P

HQ = 64
KVH = 4
HD = 128
DRAFT = 16

epsilon = 1e-06
masked_fill = -1e30
SCALE = math.log2(math.e) / math.sqrt(HD)


def rms_norm(values, gain_row):
    return (
        values * lax.rsqrt(jnp.mean(values * values, axis=-1, keepdims=True) + epsilon) * gain_row
    )


def attend_kernel(narrow_count, lengths_ref, base_ref, q_ref, k_ref, v_ref, o_ref, stats_ref):
    span = k_ref.shape[1]
    rows = q_ref.shape[2]
    per_key = narrow_count // KVH
    remaining = lengths_ref[pl.program_id(0)] - base_ref[0]
    ones = jnp.ones((span, HD), jnp.bfloat16)
    lanes = lax.broadcasted_iota(jnp.int32, (per_key * rows, HD), 1)

    def body(masked):
        stats = jnp.zeros((per_key * rows, HD), jnp.float32)
        for k in range(KVH):
            q = q_ref[k * per_key : (k + 1) * per_key, 0].reshape(per_key * rows, HD)
            keys = k_ref[0, :, k * HD : (k + 1) * HD]
            values = v_ref[0, :, k * HD : (k + 1) * HD]
            scores = lax.dot_general(
                q, keys, (((1,), (1,)), ((), ())), preferred_element_type=jnp.float32
            )
            if masked:
                live = lax.broadcasted_iota(jnp.int32, scores.shape, 1) < remaining
                scores = jnp.where(live, scores, masked_fill)
            top = jnp.max(scores, axis=1, keepdims=True) * SCALE
            weights = jnp.exp2(scores * SCALE - top).astype(jnp.bfloat16)
            both = jnp.dot(
                weights,
                jnp.concatenate([values, ones], axis=1),
                preferred_element_type=jnp.float32,
            )
            o_ref[k * per_key : (k + 1) * per_key, 0] = (
                both[:, :HD].astype(jnp.bfloat16).reshape(per_key, rows, HD)
            )
            stats = jnp.where(lanes == 2 * k, top, stats)
            stats = jnp.where(lanes == 2 * k + 1, both[:, HD:], stats)
        stats_ref[0] = stats.T[: 2 * KVH]

    @pl.when(remaining >= span)
    def _():
        body(False)

    @pl.when((remaining > 0) & (remaining < span))
    def _():
        body(True)

    @pl.when(remaining <= 0)
    def _():
        o_ref[...] = jnp.zeros_like(o_ref)
        row = lax.broadcasted_iota(jnp.int32, stats_ref.shape, 1)
        stats_ref[...] = jnp.where(row % 2 == 0, masked_fill, 0.0)


def attend(queries, cache_keys, cache_values, lengths, base):
    narrow_count, requests, rows, _ = queries.shape
    span = cache_keys.shape[1]
    per_key = narrow_count // KVH
    q_spec = pl.BlockSpec((narrow_count, 1, rows, HD), lambda r, *_: (0, r, 0, 0))
    kv_spec = pl.BlockSpec((1, span, KVH * HD), lambda r, *_: (r, 0, 0))
    return pl.pallas_call(
        functools.partial(attend_kernel, narrow_count),
        grid_spec=pltpu.PrefetchScalarGridSpec(
            num_scalar_prefetch=2,
            grid=(requests,),
            in_specs=[q_spec, kv_spec, kv_spec],
            out_specs=[
                q_spec,
                pl.BlockSpec((1, 2 * KVH, per_key * rows), lambda r, *_: (r, 0, 0)),
            ],
        ),
        out_shape=[
            jax.ShapeDtypeStruct(queries.shape, jnp.bfloat16),
            jax.ShapeDtypeStruct((requests, 2 * KVH, per_key * rows), jnp.float32),
        ],
        compiler_params=pltpu.CompilerParams(vmem_limit_bytes=48 * 1024 * 1024),
        cost_estimate=pl.CostEstimate(
            flops=4 * requests * narrow_count * rows * span * HD,
            bytes_accessed=4 * requests * span * KVH * HD,
            transcendentals=requests * narrow_count * rows * span,
        ),
    )(lengths, base, queries, cache_keys, cache_values)


def local(
    hidden,
    norm_gain,
    w_query,
    w_keyval,
    query_gain,
    key_gain,
    cache_keys,
    cache_values,
    cache_lengths,
    owner_rank,
    draft_mask,
    w_output,
):
    narrow_count = lax.axis_size("narrow")
    wide_count = lax.axis_size("wide")
    my_index = lax.axis_index("narrow")
    tok_rows, features = hidden.shape
    requests = tok_rows // DRAFT
    per_head = HQ // narrow_count
    group = HQ // KVH
    span = cache_keys.shape[1]
    per_pair = requests // wide_count
    per_key = narrow_count // KVH
    rows = per_head * DRAFT

    request_ids = jnp.arange(requests, dtype=jnp.int32)
    earlier_same = (owner_rank[:, None] == owner_rank[None, :]) & (
        request_ids[None, :] < request_ids[:, None]
    )
    rank_within = jnp.sum(earlier_same.astype(jnp.int32), axis=1)
    position = owner_rank * per_pair + rank_within
    inverse = jnp.sum(
        jnp.where(position[None, :] == request_ids[:, None], request_ids[None, :], 0), axis=1
    )

    mask_rows = jnp.pad(
        draft_mask.reshape(tok_rows, DRAFT).astype(jnp.bfloat16), ((0, 0), (0, HD - DRAFT))
    )
    packed = jnp.concatenate([hidden, mask_rows], axis=1).reshape(requests, -1)
    packed = jnp.take(packed, inverse, axis=0)
    owned = lax.all_to_all(packed, "wide", split_axis=0, concat_axis=0, tiled=True)
    owned = owned.reshape(tok_rows, features + HD)
    allowed = owned[:, features : features + DRAFT].reshape(requests, DRAFT, DRAFT) == 1

    whole = lax.all_gather(owned[:, :features], "narrow", axis=1, tiled=True)
    normed = rms_norm(whole.astype(jnp.float32), norm_gain).astype(jnp.bfloat16)
    queries = jnp.dot(normed, w_query, preferred_element_type=jnp.float32).reshape(
        requests, DRAFT, per_head, HD
    )
    queries = rms_norm(queries, query_gain).astype(jnp.bfloat16)
    own_queries = queries.transpose(0, 2, 1, 3).reshape(requests, rows, HD)
    all_queries = lax.all_gather(own_queries, "narrow", axis=0, tiled=False)

    columns = lax.dynamic_slice_in_dim(normed, my_index * features, features, 1)
    keyval = lax.psum(jnp.dot(columns, w_keyval, preferred_element_type=jnp.float32), "narrow")

    partial, stats = attend(
        all_queries,
        cache_keys,
        cache_values,
        cache_lengths,
        (my_index * span).astype(jnp.int32).reshape(1),
    )
    stats = stats.reshape(requests, KVH, 2, per_key, rows).transpose(1, 3, 0, 2, 4)
    stats = stats.reshape(narrow_count, requests, 2, rows)
    partial = lax.all_to_all(partial, "narrow", split_axis=0, concat_axis=0, tiled=True)
    stats = lax.all_to_all(stats, "narrow", split_axis=0, concat_axis=0, tiled=True)

    key_head = my_index * per_head // group
    draft_keys = lax.dynamic_slice_in_dim(keyval, key_head * HD, HD, 1)
    draft_values = lax.dynamic_slice_in_dim(keyval, (KVH + key_head) * HD, HD, 1)
    draft_keys = rms_norm(draft_keys, key_gain).astype(jnp.bfloat16).reshape(requests, DRAFT, HD)
    draft_values = draft_values.astype(jnp.bfloat16).reshape(requests, DRAFT, HD)
    draft_scores = (
        jnp.einsum("rqd,rsd->rqs", own_queries, draft_keys, preferred_element_type=jnp.float32)
        * SCALE
    )
    seen = jnp.tile(allowed, (1, per_head, 1))
    draft_scores = jnp.where(seen, draft_scores, masked_fill)
    draft_max = jnp.max(draft_scores, axis=-1)
    top = jnp.maximum(jnp.max(stats[:, :, 0], axis=0), draft_max)
    draft_weights = jnp.where(seen, jnp.exp2(draft_scores - top[..., None]), 0.0)
    draft_sum = jnp.einsum(
        "rqs,rsd->rqd",
        draft_weights.astype(jnp.bfloat16),
        draft_values,
        preferred_element_type=jnp.float32,
    )
    scaling = jnp.exp2(stats[:, :, 0] - top)
    total = jnp.sum(stats[:, :, 1] * scaling, axis=0) + jnp.sum(draft_weights, axis=-1)
    joined = jnp.sum(partial.astype(jnp.float32) * scaling[..., None], axis=0) + draft_sum
    attended = (
        (joined / total[..., None])
        .reshape(requests, per_head, DRAFT, HD)
        .transpose(0, 2, 1, 3)
        .reshape(tok_rows, per_head * HD)
        .astype(jnp.bfloat16)
    )
    terms = jnp.dot(attended, w_output, preferred_element_type=jnp.float32)
    summed = lax.psum_scatter(terms, "narrow", scatter_dimension=1, tiled=True)
    back = lax.all_to_all(
        summed.astype(jnp.bfloat16).reshape(requests, -1),
        "wide",
        split_axis=0,
        concat_axis=0,
        tiled=True,
    )
    return jnp.take(back, position, axis=0).reshape(tok_rows, features)


def solution(mesh):
    in_specs = (
        P("wide", "narrow"),
        P(),
        P(None, "narrow"),
        P("narrow", None),
        P(),
        P(),
        P("wide", "narrow", None),
        P("wide", "narrow", None),
        P("wide"),
        P("wide"),
        P("wide", None, None),
        P("narrow", None),
    )
    out_specs = P("wide", "narrow")
    return jax.shard_map(local, mesh=mesh, in_specs=in_specs, out_specs=out_specs, check_vma=False)
```

```python
import functools
import math

import jax
import jax.numpy as jnp
from jax import lax
from jax.experimental import pallas as pl
from jax.experimental.pallas import tpu as pltpu
from jax.sharding import PartitionSpec as P

HQ = 64
KVH = 4
HD = 128
DRAFT = 16

epsilon = 1e-06
masked_fill = -1e30
SCALE = math.log2(math.e) / math.sqrt(HD)


def rms_norm(values, gain_row):
    return (
        values * lax.rsqrt(jnp.mean(values * values, axis=-1, keepdims=True) + epsilon) * gain_row
    )


def attend_kernel(narrow_count, lengths_ref, base_ref, q_ref, k_ref, v_ref, o_ref, stats_ref):
    span = k_ref.shape[1]
    rows = q_ref.shape[2]
    per_key = narrow_count // KVH
    request = pl.program_id(0)
    remaining = lengths_ref[request] - base_ref[0]
    ones = jnp.ones((span, HD), jnp.bfloat16)
    lanes = lax.broadcasted_iota(jnp.int32, (per_key * rows, HD), 1)

    def body(masked):
        stats = jnp.zeros((per_key * rows, HD), jnp.float32)
        for k in range(KVH):
            q = q_ref[k * per_key : (k + 1) * per_key, 0].reshape(per_key * rows, HD)
            keys = k_ref[0, :, k * HD : (k + 1) * HD]
            values = v_ref[0, :, k * HD : (k + 1) * HD]
            scores = lax.dot_general(
                q, keys, (((1,), (1,)), ((), ())), preferred_element_type=jnp.float32
            )
            if masked:
                live = lax.broadcasted_iota(jnp.int32, scores.shape, 1) < remaining
                scores = jnp.where(live, scores, masked_fill)
            top = jnp.max(scores, axis=1, keepdims=True) * SCALE
            weights = jnp.exp2(scores * SCALE - top).astype(jnp.bfloat16)
            both = jnp.dot(
                weights,
                jnp.concatenate([values, ones], axis=1),
                preferred_element_type=jnp.float32,
            )
            o_ref[k * per_key : (k + 1) * per_key, 0] = (
                both[:, :HD].astype(jnp.bfloat16).reshape(per_key, rows, HD)
            )
            stats = jnp.where(lanes == 2 * k, top, stats)
            stats = jnp.where(lanes == 2 * k + 1, both[:, HD:], stats)
        turned = stats.T
        for k in range(KVH):
            for i in range(per_key):
                for which in range(2):
                    stats_ref[k * per_key + i, which, pl.ds(request, 1), :] = turned[
                        2 * k + which : 2 * k + which + 1, i * rows : (i + 1) * rows
                    ]

    @pl.when(remaining >= span)
    def _():
        body(False)

    @pl.when((remaining > 0) & (remaining < span))
    def _():
        body(True)

    @pl.when(remaining <= 0)
    def _():
        o_ref[...] = jnp.zeros_like(o_ref)
        for d in range(narrow_count):
            stats_ref[d, 0, pl.ds(request, 1), :] = jnp.full((1, rows), masked_fill, jnp.float32)
            stats_ref[d, 1, pl.ds(request, 1), :] = jnp.zeros((1, rows), jnp.float32)


def attend(queries, cache_keys, cache_values, lengths, base):
    narrow_count, requests, rows, _ = queries.shape
    span = cache_keys.shape[1]
    q_spec = pl.BlockSpec((narrow_count, 1, rows, HD), lambda r, *_: (0, r, 0, 0))
    kv_spec = pl.BlockSpec((1, span, KVH * HD), lambda r, *_: (r, 0, 0))
    return pl.pallas_call(
        functools.partial(attend_kernel, narrow_count),
        grid_spec=pltpu.PrefetchScalarGridSpec(
            num_scalar_prefetch=2,
            grid=(requests,),
            in_specs=[q_spec, kv_spec, kv_spec],
            out_specs=[
                q_spec,
                pl.BlockSpec(
                    (narrow_count, 2, requests, rows), lambda r, *_: (0, 0, 0, 0)
                ),
            ],
        ),
        out_shape=[
            jax.ShapeDtypeStruct(queries.shape, jnp.bfloat16),
            jax.ShapeDtypeStruct((narrow_count, 2, requests, rows), jnp.float32),
        ],
        compiler_params=pltpu.CompilerParams(vmem_limit_bytes=48 * 1024 * 1024),
        cost_estimate=pl.CostEstimate(
            flops=4 * requests * narrow_count * rows * span * HD,
            bytes_accessed=4 * requests * span * KVH * HD,
            transcendentals=requests * narrow_count * rows * span,
        ),
    )(lengths, base, queries, cache_keys, cache_values)


MIB = 1024 * 1024


def remote(src, dst, send_sem, recv_sem, wide, narrow):
    return pltpu.make_async_remote_copy(
        src_ref=src,
        dst_ref=dst,
        send_sem=send_sem,
        recv_sem=recv_sem,
        device_id=(wide, narrow),
        device_id_type=pl.DeviceIdType.MESH,
    )


def greet(peers):
    barrier = pltpu.get_barrier_semaphore()
    for peer in peers:
        pl.semaphore_signal(
            barrier, inc=1, device_id=peer, device_id_type=pl.DeviceIdType.MESH
        )
    pl.semaphore_wait(barrier, len(peers))


def slot_rows(owner_ref, token_ids, per_pair):
    requests = owner_ref.shape[0]
    owners = [owner_ref[r] for r in range(requests)]
    rows = jnp.zeros_like(token_ids)
    for r in range(requests):
        place = owners[r] * per_pair
        for earlier in range(r):
            place = place + jnp.where(owners[earlier] == owners[r], 1, 0)
        rows = jnp.where(token_ids // DRAFT == r, place * DRAFT + token_ids % DRAFT, rows)
    return rows


def gather_chips(buffer, send_sem, recv_sem, wide, me, chips, between=None):
    chip, core = me // 2, me % 2
    mate = chip * 2 + 1 - core
    sends = []

    def send(block, target, slot):
        copy = remote(
            buffer.at[block],
            buffer.at[block],
            send_sem.at[slot],
            recv_sem.at[block],
            wide,
            target,
        )
        copy.start()
        sends.append(copy)

    for off in range(1, chips):
        send(me, lax.rem(chip + off, chips) * 2 + core, off)
    send(me, mate, 0)
    if between is not None:
        between()

    def arrived(block):
        remote(
            buffer.at[block], buffer.at[block], send_sem.at[0], recv_sem.at[block], wide, mate
        ).wait_recv()

    for off in range(1, chips):
        block = lax.rem(chip - off + chips, chips) * 2 + core
        arrived(block)
        send(block, mate, chips - 1 + off)
    arrived(mate)
    for off in range(1, chips):
        arrived(lax.rem(chip - off + chips, chips) * 2 + 1 - core)
    for copy in sends:
        copy.wait_send()


def front_kernel(
    wide_count,
    narrow_count,
    owner_ref,
    hidden_ref,
    mask_ref,
    gain_ref,
    query_gain_ref,
    wq_hbm,
    wkv_ref,
    q_out,
    own_out,
    mask_out,
    kv_out,
    wq,
    staged,
    landed,
    gathered,
    q_all,
    kv_part,
    kv_land,
    kv_pair,
    wq_sem,
    a_send,
    a_recv,
    g_send,
    g_recv,
    q_send,
    q_recv,
    k_send,
    k_recv,
):
    wide, me = lax.axis_index("wide"), lax.axis_index("narrow")
    chips = narrow_count // 2
    chip, core = me // 2, me % 2
    mate = chip * 2 + 1 - core
    tokens, features = hidden_ref.shape
    requests = tokens // DRAFT
    part = tokens // wide_count
    per_head = HQ // narrow_count
    per_key = narrow_count // KVH

    load = pltpu.make_async_copy(wq_hbm, wq, wq_sem)
    load.start()
    peers = [(lax.rem(wide + off, wide_count), me) for off in range(1, wide_count)]
    peers += [(wide, lax.rem(chip + off, chips) * 2 + core) for off in range(1, chips)]
    peers += [(wide, mate)]
    greet(peers)

    target = slot_rows(
        owner_ref, lax.broadcasted_iota(jnp.int32, (tokens, tokens), 1), part // DRAFT
    )
    chosen = lax.broadcasted_iota(jnp.int32, (tokens, tokens), 0) == target
    chosen = jnp.where(chosen, 1.0, 0.0).astype(jnp.bfloat16)
    staged[:, :features] = jnp.dot(
        chosen, hidden_ref[...], preferred_element_type=jnp.float32
    ).astype(jnp.bfloat16)
    staged[:, features:] = jnp.dot(
        chosen, mask_ref[...], preferred_element_type=jnp.float32
    ).astype(jnp.bfloat16)

    sends = []
    for off in range(1, wide_count):
        there = lax.rem(wide + off, wide_count)
        copy = remote(
            staged.at[pl.ds(pl.multiple_of(there * part, part), part)],
            landed.at[wide],
            a_send.at[off],
            a_recv.at[wide],
            there,
            me,
        )
        copy.start()
        sends.append(copy)
    landed[wide] = staged[pl.ds(pl.multiple_of(wide * part, part), part)]
    for off in range(1, wide_count):
        there = lax.rem(wide - off + wide_count, wide_count)
        remote(
            landed.at[there], landed.at[there], a_send.at[0], a_recv.at[there], there, me
        ).wait_recv()
    rows = landed[...].reshape(tokens, features + tokens)
    gathered[me] = rows[:, :features]
    mask_out[...] = rows[:, features:]
    gather_chips(gathered, g_send, g_recv, wide, me, chips)
    for copy in sends:
        copy.wait_send()

    squares = jnp.zeros((tokens, 1), jnp.float32)
    for j in range(narrow_count):
        block = gathered[j].astype(jnp.float32)
        squares += jnp.sum(block * block, axis=1, keepdims=True)
    factor = lax.rsqrt(squares * (1.0 / (narrow_count * features)) + epsilon)

    def normed(j):
        return (gathered[j].astype(jnp.float32) * factor * gain_ref[j]).astype(jnp.bfloat16)

    keyval = jnp.dot(normed(me), wkv_ref[...], preferred_element_type=jnp.float32)
    for c in range(chips):
        k = c * 2 // per_key
        kv_part[c, :, :HD] = keyval[:, k * HD : (k + 1) * HD]
        kv_part[c, :, HD:] = keyval[:, (KVH + k) * HD : (KVH + k + 1) * HD]
    kv_sends = []
    for off in range(1, chips):
        there = lax.rem(chip + off, chips)
        copy = remote(
            kv_part.at[there],
            kv_land.at[chip],
            k_send.at[off],
            k_recv.at[chip],
            wide,
            there * 2 + core,
        )
        copy.start()
        kv_sends.append(copy)

    load.wait()
    total = jnp.zeros((tokens, per_head * HD), jnp.float32)
    for j in range(narrow_count):
        total += jnp.dot(
            normed(j),
            wq[j * features : (j + 1) * features, :],
            preferred_element_type=jnp.float32,
        )
    for h in range(per_head):
        one = rms_norm(total[:, h * HD : (h + 1) * HD], query_gain_ref[...]).astype(jnp.bfloat16)
        q_all[me, :, h * DRAFT : (h + 1) * DRAFT, :] = one.reshape(requests, DRAFT, HD)

    def exchange_kv():
        summed = kv_part[chip]
        for off in range(1, chips):
            there = lax.rem(chip - off + chips, chips)
            remote(
                kv_land.at[there],
                kv_land.at[there],
                k_send.at[0],
                k_recv.at[there],
                wide,
                there * 2 + core,
            ).wait_recv()
            summed = summed + kv_land[there]
        kv_pair[0] = summed
        copy = remote(
            kv_pair.at[0], kv_pair.at[1], k_send.at[0], k_recv.at[chips], wide, mate
        )
        copy.start()
        kv_sends.append(copy)

    gather_chips(q_all, q_send, q_recv, wide, me, chips, exchange_kv)
    q_out[...] = q_all[...]
    own_out[...] = q_all[me]
    remote(
        kv_pair.at[0], kv_pair.at[1], k_send.at[0], k_recv.at[chips], wide, mate
    ).wait_recv()
    kv_out[...] = kv_pair[0] + kv_pair[1]
    for copy in kv_sends:
        copy.wait_send()


def back_kernel(
    wide_count,
    narrow_count,
    owner_ref,
    q_ref,
    mask_ref,
    kv_ref,
    key_gain_ref,
    o_hbm,
    stats_hbm,
    wo_hbm,
    out_ref,
    wo,
    o_land,
    s_land,
    att,
    mate_part,
    mate_land,
    chip_part,
    chip_land,
    y,
    y_land,
    wo_sem,
    own_sem,
    o_send,
    o_recv,
    s_send,
    s_recv,
    m_send,
    m_recv,
    c_send,
    c_recv,
    y_send,
    y_recv,
):
    wide, me = lax.axis_index("wide"), lax.axis_index("narrow")
    chips = narrow_count // 2
    chip, core = me // 2, me % 2
    mate = chip * 2 + 1 - core
    requests, rows, _ = q_ref.shape
    tokens, features = out_ref.shape
    part = tokens // wide_count
    per_head = rows // DRAFT

    load = pltpu.make_async_copy(wo_hbm, wo, wo_sem)
    load.start()
    peers = [(lax.rem(wide + off, wide_count), me) for off in range(1, wide_count)]
    peers += [(wide, lax.rem(me + off, narrow_count)) for off in range(1, narrow_count)]
    greet(peers)

    sends = []
    for off in range(1, narrow_count):
        there = lax.rem(me + off, narrow_count)
        for copy in (
            remote(
                stats_hbm.at[there], s_land.at[me], s_send.at[off], s_recv.at[me], wide, there
            ),
            remote(o_hbm.at[there], o_land.at[me], o_send.at[off], o_recv.at[me], wide, there),
        ):
            copy.start()
            sends.append(copy)
    own = [
        pltpu.make_async_copy(stats_hbm.at[me], s_land.at[me], own_sem.at[0]),
        pltpu.make_async_copy(o_hbm.at[me], o_land.at[me], own_sem.at[1]),
    ]
    for copy in own:
        copy.start()

    draft_keys = rms_norm(kv_ref[:, :HD], key_gain_ref[...]).astype(jnp.bfloat16)
    draft_values = kv_ref[:, HD:].astype(jnp.bfloat16)
    request_of = lax.broadcasted_iota(jnp.int32, (rows, tokens), 1) // DRAFT
    drafts = []
    for r in range(requests):
        scores = (
            lax.dot_general(
                q_ref[r], draft_keys, (((1,), (1,)), ((), ())), preferred_element_type=jnp.float32
            )
            * SCALE
        )
        mask = mask_ref[r * DRAFT : (r + 1) * DRAFT, :].astype(jnp.float32)
        seen = (jnp.concatenate([mask] * per_head, axis=0) == 1.0) & (request_of == r)
        scores = jnp.where(seen, scores, masked_fill)
        top = jnp.max(scores, axis=1, keepdims=True)
        weights = jnp.where(seen, jnp.exp2(scores - top), 0.0)
        total = jnp.sum(weights, axis=1, keepdims=True)
        summed = jnp.dot(
            weights.astype(jnp.bfloat16), draft_values, preferred_element_type=jnp.float32
        )
        drafts.append((top, total, summed))

    for copy in own:
        copy.wait()
    for off in range(1, narrow_count):
        there = lax.rem(me - off + narrow_count, narrow_count)
        remote(
            s_land.at[there], s_land.at[there], s_send.at[0], s_recv.at[there], wide, there
        ).wait_recv()
        remote(
            o_land.at[there], o_land.at[there], o_send.at[0], o_recv.at[there], wide, there
        ).wait_recv()

    tops = s_land[0, 0]
    for j in range(1, narrow_count):
        tops = jnp.maximum(tops, s_land[j, 0])
    scaling = [jnp.exp2(s_land[j, 0] - tops) for j in range(narrow_count)]
    totals = scaling[0] * s_land[0, 1]
    for j in range(1, narrow_count):
        totals = totals + scaling[j] * s_land[j, 1]
    listed = jnp.concatenate(scaling + [tops, totals], axis=0)
    filled = -(-listed.shape[0] // 128) * 128
    if filled > listed.shape[0]:
        listed = jnp.concatenate(
            [listed, jnp.zeros((filled - listed.shape[0], rows), jnp.float32)], axis=0
        )
    turned = listed.T

    def column(which, r):
        place = which * requests + r
        return turned[:, place : place + 1]

    for r in range(requests):
        draft_top, draft_total, joined = drafts[r]
        cache_top = column(narrow_count, r)
        top = jnp.maximum(cache_top, draft_top)
        cache_scale, draft_scale = jnp.exp2(cache_top - top), jnp.exp2(draft_top - top)
        summed = column(0, r) * o_land[0, r].astype(jnp.float32)
        for j in range(1, narrow_count):
            summed = summed + column(j, r) * o_land[j, r].astype(jnp.float32)
        total = column(narrow_count + 1, r) * cache_scale + draft_total * draft_scale
        value = ((summed * cache_scale + joined * draft_scale) / total).astype(jnp.bfloat16)
        for h in range(per_head):
            att[r * DRAFT : (r + 1) * DRAFT, h * HD : (h + 1) * HD] = value[
                h * DRAFT : (h + 1) * DRAFT
            ]

    load.wait()

    def terms(device):
        place = pl.ds(pl.multiple_of(device * features, features), features)
        return jnp.dot(att[...], wo[:, place], preferred_element_type=jnp.float32)

    for step in range(1, chips + 1):
        there = lax.rem(chip + step, chips)
        mate_part[there] = terms(there * 2 + 1 - core).astype(jnp.bfloat16)
        copy = remote(
            mate_part.at[there],
            mate_land.at[there],
            m_send.at[there],
            m_recv.at[there],
            wide,
            mate,
        )
        copy.start()
        sends.append(copy)
    summed = None
    for step in range(1, chips + 1):
        there = lax.rem(chip + step, chips)
        value = terms(there * 2 + core)
        remote(
            mate_land.at[there], mate_land.at[there], m_send.at[0], m_recv.at[there], wide, mate
        ).wait_recv()
        value = value + mate_land[there].astype(jnp.float32)
        if step < chips:
            chip_part[there] = value.astype(jnp.bfloat16)
            copy = remote(
                chip_part.at[there],
                chip_land.at[chip],
                c_send.at[there],
                c_recv.at[chip],
                wide,
                there * 2 + core,
            )
            copy.start()
            sends.append(copy)
        else:
            summed = value
    for off in range(1, chips):
        there = lax.rem(chip - off + chips, chips)
        remote(
            chip_land.at[there],
            chip_land.at[there],
            c_send.at[0],
            c_recv.at[there],
            wide,
            there * 2 + core,
        ).wait_recv()
        summed = summed + chip_land[there].astype(jnp.float32)
    y[...] = summed.astype(jnp.bfloat16)

    for off in range(1, wide_count):
        there = lax.rem(wide + off, wide_count)
        copy = remote(
            y.at[pl.ds(pl.multiple_of(there * part, part), part)],
            y_land.at[wide],
            y_send.at[off],
            y_recv.at[wide],
            there,
            me,
        )
        copy.start()
        sends.append(copy)
    y_land[wide] = y[pl.ds(pl.multiple_of(wide * part, part), part)]
    source = slot_rows(
        owner_ref, lax.broadcasted_iota(jnp.int32, (tokens, tokens), 0), part // DRAFT
    )
    chosen = lax.broadcasted_iota(jnp.int32, (tokens, tokens), 1) == source
    chosen = jnp.where(chosen, 1.0, 0.0).astype(jnp.bfloat16)
    for off in range(1, wide_count):
        there = lax.rem(wide - off + wide_count, wide_count)
        remote(
            y_land.at[there], y_land.at[there], y_send.at[0], y_recv.at[there], there, me
        ).wait_recv()
    out_ref[...] = jnp.dot(
        chosen, y_land[...].reshape(tokens, features), preferred_element_type=jnp.float32
    ).astype(jnp.bfloat16)
    for copy in sends:
        copy.wait_send()


def local(
    hidden,
    norm_gain,
    w_query,
    w_keyval,
    query_gain,
    key_gain,
    cache_keys,
    cache_values,
    cache_lengths,
    owner_rank,
    draft_mask,
    w_output,
):
    narrow_count = lax.axis_size("narrow")
    wide_count = lax.axis_size("wide")
    tokens, features = hidden.shape
    requests = tokens // DRAFT
    per_head = HQ // narrow_count
    span = cache_keys.shape[1]
    part = tokens // wide_count
    chips = narrow_count // 2
    rows = per_head * DRAFT
    vmem = pl.BlockSpec(memory_space=pltpu.VMEM)
    smem = pl.BlockSpec(memory_space=pltpu.SMEM)
    anywhere = pl.BlockSpec(memory_space=pl.ANY)
    dma = pltpu.SemaphoreType.DMA
    bf16, f32 = jnp.bfloat16, jnp.float32

    mask_rows = jnp.tile(draft_mask.reshape(tokens, DRAFT).astype(bf16), (1, tokens // DRAFT))
    all_queries, own_queries, owned_mask, keyval = pl.pallas_call(
        functools.partial(front_kernel, wide_count, narrow_count),
        out_shape=[
            jax.ShapeDtypeStruct((narrow_count, requests, rows, HD), bf16),
            jax.ShapeDtypeStruct((requests, rows, HD), bf16),
            jax.ShapeDtypeStruct((tokens, tokens), bf16),
            jax.ShapeDtypeStruct((tokens, 2 * HD), f32),
        ],
        in_specs=[smem, vmem, vmem, vmem, vmem, anywhere, vmem],
        out_specs=[vmem] * 4,
        scratch_shapes=[
            pltpu.VMEM(w_query.shape, bf16),
            pltpu.VMEM((tokens, features + tokens), bf16),
            pltpu.VMEM((wide_count, part, features + tokens), bf16),
            pltpu.VMEM((narrow_count, tokens, features), bf16),
            pltpu.VMEM((narrow_count, requests, rows, HD), bf16),
            pltpu.VMEM((chips, tokens, 2 * HD), f32),
            pltpu.VMEM((chips, tokens, 2 * HD), f32),
            pltpu.VMEM((2, tokens, 2 * HD), f32),
            dma,
            dma((wide_count,)),
            dma((wide_count,)),
            dma((narrow_count,)),
            dma((narrow_count,)),
            dma((narrow_count,)),
            dma((narrow_count,)),
            dma((chips,)),
            dma((chips + 1,)),
        ],
        compiler_params=pltpu.CompilerParams(
            collective_id=0, has_side_effects=True, vmem_limit_bytes=40 * MIB
        ),
    )(
        owner_rank,
        hidden,
        mask_rows,
        norm_gain.reshape(narrow_count, 1, features),
        query_gain.reshape(1, HD),
        w_query,
        w_keyval,
    )

    base = (lax.axis_index("narrow") * span).astype(jnp.int32).reshape(1)
    partial, stats = attend(all_queries, cache_keys, cache_values, cache_lengths, base)

    return pl.pallas_call(
        functools.partial(back_kernel, wide_count, narrow_count),
        out_shape=jax.ShapeDtypeStruct((tokens, features), bf16),
        in_specs=[smem, vmem, vmem, vmem, vmem, anywhere, anywhere, anywhere],
        out_specs=vmem,
        scratch_shapes=[
            pltpu.VMEM(w_output.shape, bf16),
            pltpu.VMEM((narrow_count, requests, rows, HD), bf16),
            pltpu.VMEM((narrow_count, 2, requests, rows), f32),
            pltpu.VMEM((tokens, per_head * HD), bf16),
            pltpu.VMEM((chips, tokens, features), bf16),
            pltpu.VMEM((chips, tokens, features), bf16),
            pltpu.VMEM((chips, tokens, features), bf16),
            pltpu.VMEM((chips, tokens, features), bf16),
            pltpu.VMEM((tokens, features), bf16),
            pltpu.VMEM((wide_count, part, features), bf16),
            dma,
            dma((2,)),
            dma((narrow_count,)),
            dma((narrow_count,)),
            dma((narrow_count,)),
            dma((narrow_count,)),
            dma((chips,)),
            dma((chips,)),
            dma((chips,)),
            dma((chips,)),
            dma((wide_count,)),
            dma((wide_count,)),
        ],
        compiler_params=pltpu.CompilerParams(
            collective_id=1, has_side_effects=True, vmem_limit_bytes=40 * MIB
        ),
    )(
        owner_rank,
        own_queries,
        owned_mask,
        keyval,
        key_gain.reshape(1, HD),
        partial,
        stats,
        w_output,
    )


def solution(mesh):
    in_specs = (
        P("wide", "narrow"),
        P(),
        P(None, "narrow"),
        P("narrow", None),
        P(),
        P(),
        P("wide", "narrow", None),
        P("wide", "narrow", None),
        P("wide"),
        P("wide"),
        P("wide", None, None),
        P("narrow", None),
    )
    out_specs = P("wide", "narrow")
    return jax.shard_map(local, mesh=mesh, in_specs=in_specs, out_specs=out_specs, check_vma=False)
```

```python
import functools
import math

import jax
import jax.numpy as jnp
from jax import lax
from jax.experimental import pallas as pl
from jax.experimental.pallas import tpu as pltpu
from jax.sharding import PartitionSpec as P

HQ = 64
KVH = 4
HD = 128
DRAFT = 16

epsilon = 1e-06
masked_fill = -1e30
SCALE = math.log2(math.e) / math.sqrt(HD)


def rms_norm(values, gain_row):
    return (
        values * lax.rsqrt(jnp.mean(values * values, axis=-1, keepdims=True) + epsilon) * gain_row
    )


MIB = 1024 * 1024
PAIR = 2


def remote(src, dst, send_sem, recv_sem, wide, narrow):
    return pltpu.make_async_remote_copy(
        src_ref=src,
        dst_ref=dst,
        send_sem=send_sem,
        recv_sem=recv_sem,
        device_id=(wide, narrow),
        device_id_type=pl.DeviceIdType.MESH,
    )


def greet(peers):
    barrier = pltpu.get_barrier_semaphore()
    for peer in peers:
        pl.semaphore_signal(
            barrier, inc=1, device_id=peer, device_id_type=pl.DeviceIdType.MESH
        )
    pl.semaphore_wait(barrier, len(peers))


def slot_rows(owner_ref, token_ids, per_pair):
    requests = owner_ref.shape[0]
    owners = [owner_ref[r] for r in range(requests)]
    rows = jnp.zeros_like(token_ids)
    for r in range(requests):
        place = owners[r] * per_pair
        for earlier in range(r):
            place = place + jnp.where(owners[earlier] == owners[r], 1, 0)
        rows = jnp.where(token_ids // DRAFT == r, place * DRAFT + token_ids % DRAFT, rows)
    return rows


def gather_chips(buffer, send_sem, recv_sem, wide, me, chips, between=None):
    chip, core = me // 2, me % 2
    mate = chip * 2 + 1 - core
    sends = []

    def send(block, target, slot):
        copy = remote(
            buffer.at[block],
            buffer.at[block],
            send_sem.at[slot],
            recv_sem.at[block],
            wide,
            target,
        )
        copy.start()
        sends.append(copy)

    for off in range(1, chips):
        send(me, lax.rem(chip + off, chips) * 2 + core, off)
    send(me, mate, 0)
    if between is not None:
        between()

    def arrived(block):
        remote(
            buffer.at[block], buffer.at[block], send_sem.at[0], recv_sem.at[block], wide, mate
        ).wait_recv()

    for off in range(1, chips):
        block = lax.rem(chip - off + chips, chips) * 2 + core
        arrived(block)
        send(block, mate, chips - 1 + off)
    arrived(mate)
    for off in range(1, chips):
        arrived(lax.rem(chip - off + chips, chips) * 2 + 1 - core)
    for copy in sends:
        copy.wait_send()


def front_kernel(
    wide_count,
    narrow_count,
    owner_ref,
    hidden_hbm,
    mask_hbm,
    gain_hbm,
    query_gain_hbm,
    wkv_hbm,
    wq_hbm,
    q_out,
    mask_out,
    kv_out,
    hidden_ref,
    mask_ref,
    gain_ref,
    query_gain_ref,
    wkv_ref,
    wq,
    staged,
    landed,
    gathered,
    q_all,
    kv_part,
    kv_land,
    kv_pair,
    small_sem,
    wq_sem,
    a_send,
    a_recv,
    g_send,
    g_recv,
    q_send,
    q_recv,
    k_send,
    k_recv,
):
    wide, me = lax.axis_index("wide"), lax.axis_index("narrow")
    chips = narrow_count // 2
    chip, core = me // 2, me % 2
    mate = chip * 2 + 1 - core
    tokens, features = hidden_ref.shape
    requests = tokens // DRAFT
    part = tokens // wide_count
    per_head = HQ // narrow_count
    per_key = narrow_count // KVH

    small = [
        pltpu.make_async_copy(source, held, small_sem.at[i])
        for i, (source, held) in enumerate(
            [
                (hidden_hbm, hidden_ref),
                (mask_hbm, mask_ref),
                (gain_hbm, gain_ref),
                (query_gain_hbm, query_gain_ref),
                (wkv_hbm, wkv_ref),
            ]
        )
    ]
    load = pltpu.make_async_copy(wq_hbm, wq, wq_sem)
    for copy in small + [load]:
        copy.start()
    peers = [(lax.rem(wide + off, wide_count), me) for off in range(1, wide_count)]
    peers += [(wide, lax.rem(chip + off, chips) * 2 + core) for off in range(1, chips)]
    peers += [(wide, mate)]
    greet(peers)
    for copy in small[:2]:
        copy.wait()

    target = slot_rows(
        owner_ref, lax.broadcasted_iota(jnp.int32, (tokens, tokens), 1), part // DRAFT
    )
    chosen = lax.broadcasted_iota(jnp.int32, (tokens, tokens), 0) == target
    chosen = jnp.where(chosen, 1.0, 0.0).astype(jnp.bfloat16)
    staged[:, :features] = jnp.dot(
        chosen, hidden_ref[...], preferred_element_type=jnp.float32
    ).astype(jnp.bfloat16)
    staged[:, features:] = jnp.dot(
        chosen, mask_ref[...], preferred_element_type=jnp.float32
    ).astype(jnp.bfloat16)

    sends = []
    for off in range(1, wide_count):
        there = lax.rem(wide + off, wide_count)
        copy = remote(
            staged.at[pl.ds(pl.multiple_of(there * part, part), part)],
            landed.at[wide],
            a_send.at[off],
            a_recv.at[wide],
            there,
            me,
        )
        copy.start()
        sends.append(copy)
    landed[wide] = staged[pl.ds(pl.multiple_of(wide * part, part), part)]
    for off in range(1, wide_count):
        there = lax.rem(wide - off + wide_count, wide_count)
        remote(
            landed.at[there], landed.at[there], a_send.at[0], a_recv.at[there], there, me
        ).wait_recv()
    rows = landed[...].reshape(tokens, features + tokens)
    gathered[me] = rows[:, :features]
    mask_out[...] = rows[:, features:]
    gather_chips(gathered, g_send, g_recv, wide, me, chips)
    for copy in sends:
        copy.wait_send()

    for copy in small[2:]:
        copy.wait()
    squares = jnp.zeros((tokens, 1), jnp.float32)
    for j in range(narrow_count):
        block = gathered[j].astype(jnp.float32)
        squares += jnp.sum(block * block, axis=1, keepdims=True)
    factor = lax.rsqrt(squares * (1.0 / (narrow_count * features)) + epsilon)

    def normed(j):
        return (gathered[j].astype(jnp.float32) * factor * gain_ref[j]).astype(jnp.bfloat16)

    keyval = jnp.dot(normed(me), wkv_ref[...], preferred_element_type=jnp.float32)
    for c in range(chips):
        k = c * 2 // per_key
        kv_part[c, :, :HD] = keyval[:, k * HD : (k + 1) * HD]
        kv_part[c, :, HD:] = keyval[:, (KVH + k) * HD : (KVH + k + 1) * HD]
    kv_sends = []
    for off in range(1, chips):
        there = lax.rem(chip + off, chips)
        copy = remote(
            kv_part.at[there],
            kv_land.at[chip],
            k_send.at[off],
            k_recv.at[chip],
            wide,
            there * 2 + core,
        )
        copy.start()
        kv_sends.append(copy)

    load.wait()
    total = jnp.zeros((tokens, per_head * HD), jnp.float32)
    for j in range(narrow_count):
        total += jnp.dot(
            normed(j),
            wq[j * features : (j + 1) * features, :],
            preferred_element_type=jnp.float32,
        )
    for h in range(per_head):
        one = rms_norm(total[:, h * HD : (h + 1) * HD], query_gain_ref[...]).astype(jnp.bfloat16)
        q_all[me, :, h * DRAFT : (h + 1) * DRAFT, :] = one.reshape(requests, DRAFT, HD)

    def exchange_kv():
        summed = kv_part[chip]
        for off in range(1, chips):
            there = lax.rem(chip - off + chips, chips)
            remote(
                kv_land.at[there],
                kv_land.at[there],
                k_send.at[0],
                k_recv.at[there],
                wide,
                there * 2 + core,
            ).wait_recv()
            summed = summed + kv_land[there]
        kv_pair[0] = summed
        copy = remote(
            kv_pair.at[0], kv_pair.at[1], k_send.at[0], k_recv.at[chips], wide, mate
        )
        copy.start()
        kv_sends.append(copy)

    gather_chips(q_all, q_send, q_recv, wide, me, chips, exchange_kv)
    q_out[...] = q_all[...]
    remote(
        kv_pair.at[0], kv_pair.at[1], k_send.at[0], k_recv.at[chips], wide, mate
    ).wait_recv()
    kv_out[...] = kv_pair[0] + kv_pair[1]
    for copy in kv_sends:
        copy.wait_send()


def back_kernel(
    wide_count,
    narrow_count,
    owner_ref,
    lengths_ref,
    q_ref,
    mask_ref,
    kv_ref,
    key_gain_ref,
    k_hbm,
    v_hbm,
    wo_hbm,
    out_ref,
    wo,
    o_part,
    s_part,
    columns,
    o_land,
    s_land,
    att,
    mate_part,
    mate_land,
    chip_part,
    chip_land,
    y,
    y_land,
    wo_sem,
    o_send,
    o_recv,
    s_send,
    s_recv,
    m_send,
    m_recv,
    c_send,
    c_recv,
    y_send,
    y_recv,
):
    wide, me = lax.axis_index("wide"), lax.axis_index("narrow")
    chips = narrow_count // 2
    chip, core = me // 2, me % 2
    mate = chip * 2 + 1 - core
    _, requests, rows, _ = q_ref.shape
    tokens, features = out_ref.shape
    part = tokens // wide_count
    per_head = rows // DRAFT

    load = pltpu.make_async_copy(wo_hbm, wo, wo_sem)
    load.start()
    peers = [(lax.rem(wide + off, wide_count), me) for off in range(1, wide_count)]
    peers += [(wide, lax.rem(me + off, narrow_count)) for off in range(1, narrow_count)]
    greet(peers)

    sends = []
    span = k_hbm.shape[1]
    per_key = narrow_count // KVH
    my_key = me // per_key
    lanes = lax.broadcasted_iota(jnp.int32, (per_key * rows, HD), 1)
    ones = jnp.ones((span, HD), jnp.bfloat16)

    def send(there):
        for copy in (
            remote(
                s_part.at[there], s_land.at[me], s_send.at[there], s_recv.at[me], wide, there
            ),
            remote(
                o_part.at[there], o_land.at[me], o_send.at[there], o_recv.at[me], wide, there
            ),
        ):
            copy.start()
            sends.append(copy)

    for step in range(1, KVH + 1):
        key = lax.rem(my_key + step, KVH)
        first = key * per_key

        def body(k_ref, v_ref, first=first):
            for i in range(PAIR):
                r = pl.program_id(0) * PAIR + i
                q = jnp.concatenate([q_ref[first + d, r] for d in range(per_key)], axis=0)
                scores = lax.dot_general(
                    q, k_ref[i], (((1,), (1,)), ((), ())), preferred_element_type=jnp.float32
                )
                remaining = lengths_ref[r] - me * span
                live = lax.broadcasted_iota(jnp.int32, scores.shape, 1) < remaining
                scores = jnp.where(live, scores, masked_fill)
                top = jnp.max(scores, axis=1, keepdims=True) * SCALE
                weights = jnp.exp2(scores * SCALE - top).astype(jnp.bfloat16)
                both = jnp.dot(
                    weights,
                    jnp.concatenate([v_ref[i], ones], axis=1),
                    preferred_element_type=jnp.float32,
                )
                for d in range(per_key):
                    o_part[first + d, r] = both[d * rows : (d + 1) * rows, :HD].astype(
                        jnp.bfloat16
                    )
                held = jnp.where(lanes == r, top, columns[...])
                columns[...] = jnp.where(lanes == requests + r, both[:, HD:], held)

        columns[...] = jnp.zeros_like(columns)
        spec = pl.BlockSpec((PAIR, span, HD), lambda r, key=key: (r, 0, key))
        pltpu.emit_pipeline(body, grid=(requests // PAIR,), in_specs=[spec, spec])(k_hbm, v_hbm)
        turned = columns[...].T
        for d in range(per_key):
            for which in range(2):
                s_part[first + d, which] = turned[
                    which * requests : (which + 1) * requests, d * rows : (d + 1) * rows
                ]
        if step < KVH:
            for d in range(per_key):
                send(first + d)
        else:
            for off in range(1, per_key):
                send(first + lax.rem(me - first + off, per_key))
    s_land[me] = s_part[me]
    o_land[me] = o_part[me]

    draft_keys = rms_norm(kv_ref[:, :HD], key_gain_ref[...]).astype(jnp.bfloat16)
    draft_values = kv_ref[:, HD:].astype(jnp.bfloat16)
    request_of = lax.broadcasted_iota(jnp.int32, (rows, tokens), 1) // DRAFT
    drafts = []
    for r in range(requests):
        scores = (
            lax.dot_general(
                q_ref[me, r], draft_keys, (((1,), (1,)), ((), ())), preferred_element_type=jnp.float32
            )
            * SCALE
        )
        mask = mask_ref[r * DRAFT : (r + 1) * DRAFT, :].astype(jnp.float32)
        seen = (jnp.concatenate([mask] * per_head, axis=0) == 1.0) & (request_of == r)
        scores = jnp.where(seen, scores, masked_fill)
        top = jnp.max(scores, axis=1, keepdims=True)
        weights = jnp.where(seen, jnp.exp2(scores - top), 0.0)
        total = jnp.sum(weights, axis=1, keepdims=True)
        summed = jnp.dot(
            weights.astype(jnp.bfloat16), draft_values, preferred_element_type=jnp.float32
        )
        drafts.append((top, total, summed))

    for off in range(1, narrow_count):
        there = lax.rem(me - off + narrow_count, narrow_count)
        remote(
            s_land.at[there], s_land.at[there], s_send.at[0], s_recv.at[there], wide, there
        ).wait_recv()
        remote(
            o_land.at[there], o_land.at[there], o_send.at[0], o_recv.at[there], wide, there
        ).wait_recv()

    tops = s_land[0, 0]
    for j in range(1, narrow_count):
        tops = jnp.maximum(tops, s_land[j, 0])
    scaling = [jnp.exp2(s_land[j, 0] - tops) for j in range(narrow_count)]
    totals = scaling[0] * s_land[0, 1]
    for j in range(1, narrow_count):
        totals = totals + scaling[j] * s_land[j, 1]
    listed = jnp.concatenate(scaling + [tops, totals], axis=0)
    filled = -(-listed.shape[0] // 128) * 128
    if filled > listed.shape[0]:
        listed = jnp.concatenate(
            [listed, jnp.zeros((filled - listed.shape[0], rows), jnp.float32)], axis=0
        )
    turned = listed.T

    def column(which, r):
        place = which * requests + r
        return turned[:, place : place + 1]

    for r in range(requests):
        draft_top, draft_total, joined = drafts[r]
        cache_top = column(narrow_count, r)
        top = jnp.maximum(cache_top, draft_top)
        cache_scale, draft_scale = jnp.exp2(cache_top - top), jnp.exp2(draft_top - top)
        summed = column(0, r) * o_land[0, r].astype(jnp.float32)
        for j in range(1, narrow_count):
            summed = summed + column(j, r) * o_land[j, r].astype(jnp.float32)
        total = column(narrow_count + 1, r) * cache_scale + draft_total * draft_scale
        value = ((summed * cache_scale + joined * draft_scale) / total).astype(jnp.bfloat16)
        for h in range(per_head):
            att[r * DRAFT : (r + 1) * DRAFT, h * HD : (h + 1) * HD] = value[
                h * DRAFT : (h + 1) * DRAFT
            ]

    load.wait()

    def terms(device):
        place = pl.ds(pl.multiple_of(device * features, features), features)
        return jnp.dot(att[...], wo[:, place], preferred_element_type=jnp.float32)

    for step in range(1, chips + 1):
        there = lax.rem(chip + step, chips)
        mate_part[there] = terms(there * 2 + 1 - core).astype(jnp.bfloat16)
        copy = remote(
            mate_part.at[there],
            mate_land.at[there],
            m_send.at[there],
            m_recv.at[there],
            wide,
            mate,
        )
        copy.start()
        sends.append(copy)
    summed = None
    for step in range(1, chips + 1):
        there = lax.rem(chip + step, chips)
        value = terms(there * 2 + core)
        remote(
            mate_land.at[there], mate_land.at[there], m_send.at[0], m_recv.at[there], wide, mate
        ).wait_recv()
        value = value + mate_land[there].astype(jnp.float32)
        if step < chips:
            chip_part[there] = value.astype(jnp.bfloat16)
            copy = remote(
                chip_part.at[there],
                chip_land.at[chip],
                c_send.at[there],
                c_recv.at[chip],
                wide,
                there * 2 + core,
            )
            copy.start()
            sends.append(copy)
        else:
            summed = value
    for off in range(1, chips):
        there = lax.rem(chip - off + chips, chips)
        remote(
            chip_land.at[there],
            chip_land.at[there],
            c_send.at[0],
            c_recv.at[there],
            wide,
            there * 2 + core,
        ).wait_recv()
        summed = summed + chip_land[there].astype(jnp.float32)
    y[...] = summed.astype(jnp.bfloat16)

    for off in range(1, wide_count):
        there = lax.rem(wide + off, wide_count)
        copy = remote(
            y.at[pl.ds(pl.multiple_of(there * part, part), part)],
            y_land.at[wide],
            y_send.at[off],
            y_recv.at[wide],
            there,
            me,
        )
        copy.start()
        sends.append(copy)
    y_land[wide] = y[pl.ds(pl.multiple_of(wide * part, part), part)]
    source = slot_rows(
        owner_ref, lax.broadcasted_iota(jnp.int32, (tokens, tokens), 0), part // DRAFT
    )
    chosen = lax.broadcasted_iota(jnp.int32, (tokens, tokens), 1) == source
    chosen = jnp.where(chosen, 1.0, 0.0).astype(jnp.bfloat16)
    for off in range(1, wide_count):
        there = lax.rem(wide - off + wide_count, wide_count)
        remote(
            y_land.at[there], y_land.at[there], y_send.at[0], y_recv.at[there], there, me
        ).wait_recv()
    out_ref[...] = jnp.dot(
        chosen, y_land[...].reshape(tokens, features), preferred_element_type=jnp.float32
    ).astype(jnp.bfloat16)
    for copy in sends:
        copy.wait_send()


def local(
    hidden,
    norm_gain,
    w_query,
    w_keyval,
    query_gain,
    key_gain,
    cache_keys,
    cache_values,
    cache_lengths,
    owner_rank,
    draft_mask,
    w_output,
):
    narrow_count = lax.axis_size("narrow")
    wide_count = lax.axis_size("wide")
    tokens, features = hidden.shape
    requests = tokens // DRAFT
    per_head = HQ // narrow_count
    part = tokens // wide_count
    chips = narrow_count // 2
    rows = per_head * DRAFT
    vmem = pl.BlockSpec(memory_space=pltpu.VMEM)
    smem = pl.BlockSpec(memory_space=pltpu.SMEM)
    anywhere = pl.BlockSpec(memory_space=pl.ANY)
    dma = pltpu.SemaphoreType.DMA
    bf16, f32 = jnp.bfloat16, jnp.float32

    mask_rows = jnp.tile(draft_mask.reshape(tokens, DRAFT).astype(bf16), (1, tokens // DRAFT))
    all_queries, owned_mask, keyval = pl.pallas_call(
        functools.partial(front_kernel, wide_count, narrow_count),
        out_shape=[
            jax.ShapeDtypeStruct((narrow_count, requests, rows, HD), bf16),
            jax.ShapeDtypeStruct((tokens, tokens), bf16),
            jax.ShapeDtypeStruct((tokens, 2 * HD), f32),
        ],
        in_specs=[smem] + [anywhere] * 6,
        out_specs=[vmem] * 3,
        scratch_shapes=[
            pltpu.VMEM(hidden.shape, bf16),
            pltpu.VMEM((tokens, tokens), bf16),
            pltpu.VMEM((narrow_count, 1, features), f32),
            pltpu.VMEM((1, HD), f32),
            pltpu.VMEM(w_keyval.shape, bf16),
            pltpu.VMEM(w_query.shape, bf16),
            pltpu.VMEM((tokens, features + tokens), bf16),
            pltpu.VMEM((wide_count, part, features + tokens), bf16),
            pltpu.VMEM((narrow_count, tokens, features), bf16),
            pltpu.VMEM((narrow_count, requests, rows, HD), bf16),
            pltpu.VMEM((chips, tokens, 2 * HD), f32),
            pltpu.VMEM((chips, tokens, 2 * HD), f32),
            pltpu.VMEM((2, tokens, 2 * HD), f32),
            dma((5,)),
            dma,
            dma((wide_count,)),
            dma((wide_count,)),
            dma((narrow_count,)),
            dma((narrow_count,)),
            dma((narrow_count,)),
            dma((narrow_count,)),
            dma((chips,)),
            dma((chips + 1,)),
        ],
        compiler_params=pltpu.CompilerParams(
            collective_id=0, has_side_effects=True, vmem_limit_bytes=56 * MIB
        ),
    )(
        owner_rank,
        hidden,
        mask_rows,
        norm_gain.reshape(narrow_count, 1, features),
        query_gain.reshape(1, HD),
        w_keyval,
        w_query,
    )

    return pl.pallas_call(
        functools.partial(back_kernel, wide_count, narrow_count),
        out_shape=jax.ShapeDtypeStruct((tokens, features), bf16),
        in_specs=[smem, smem, vmem, vmem, vmem, vmem, anywhere, anywhere, anywhere],
        out_specs=vmem,
        scratch_shapes=[
            pltpu.VMEM(w_output.shape, bf16),
            pltpu.VMEM((narrow_count, requests, rows, HD), bf16),
            pltpu.VMEM((narrow_count, 2, requests, rows), f32),
            pltpu.VMEM((narrow_count // KVH * rows, HD), f32),
            pltpu.VMEM((narrow_count, requests, rows, HD), bf16),
            pltpu.VMEM((narrow_count, 2, requests, rows), f32),
            pltpu.VMEM((tokens, per_head * HD), bf16),
            pltpu.VMEM((chips, tokens, features), bf16),
            pltpu.VMEM((chips, tokens, features), bf16),
            pltpu.VMEM((chips, tokens, features), bf16),
            pltpu.VMEM((chips, tokens, features), bf16),
            pltpu.VMEM((tokens, features), bf16),
            pltpu.VMEM((wide_count, part, features), bf16),
            dma,
            dma((narrow_count,)),
            dma((narrow_count,)),
            dma((narrow_count,)),
            dma((narrow_count,)),
            dma((chips,)),
            dma((chips,)),
            dma((chips,)),
            dma((chips,)),
            dma((wide_count,)),
            dma((wide_count,)),
        ],
        compiler_params=pltpu.CompilerParams(
            collective_id=1, has_side_effects=True, vmem_limit_bytes=56 * MIB
        ),
    )(
        owner_rank,
        cache_lengths,
        all_queries,
        owned_mask,
        keyval,
        key_gain.reshape(1, HD),
        cache_keys,
        cache_values,
        w_output,
    )


def solution(mesh):
    in_specs = (
        P("wide", "narrow"),
        P(),
        P(None, "narrow"),
        P("narrow", None),
        P(),
        P(),
        P("wide", "narrow", None),
        P("wide", "narrow", None),
        P("wide"),
        P("wide"),
        P("wide", None, None),
        P("narrow", None),
    )
    out_specs = P("wide", "narrow")
    return jax.shard_map(local, mesh=mesh, in_specs=in_specs, out_specs=out_specs, check_vma=False)
```

```python
import functools
import math

import jax
import jax.numpy as jnp
from jax import lax
from jax.experimental import pallas as pl
from jax.experimental.pallas import tpu as pltpu
from jax.sharding import PartitionSpec as P

HQ = 64
KVH = 4
HD = 128
DRAFT = 16

epsilon = 1e-06
masked_fill = -1e30
SCALE = math.log2(math.e) / math.sqrt(HD)


def rms_norm(values, gain_row):
    return (
        values * lax.rsqrt(jnp.mean(values * values, axis=-1, keepdims=True) + epsilon) * gain_row
    )


MIB = 1024 * 1024
PAIR = 2


def remote(src, dst, send_sem, recv_sem, wide, narrow):
    return pltpu.make_async_remote_copy(
        src_ref=src,
        dst_ref=dst,
        send_sem=send_sem,
        recv_sem=recv_sem,
        device_id=(wide, narrow),
        device_id_type=pl.DeviceIdType.MESH,
    )


def greet(peers):
    barrier = pltpu.get_barrier_semaphore()
    for peer in peers:
        pl.semaphore_signal(
            barrier, inc=1, device_id=peer, device_id_type=pl.DeviceIdType.MESH
        )
    pl.semaphore_wait(barrier, len(peers))


def slot_rows(owner_ref, token_ids, per_pair):
    requests = owner_ref.shape[0]
    owners = [owner_ref[r] for r in range(requests)]
    rows = jnp.zeros_like(token_ids)
    for r in range(requests):
        place = owners[r] * per_pair
        for earlier in range(r):
            place = place + jnp.where(owners[earlier] == owners[r], 1, 0)
        rows = jnp.where(token_ids // DRAFT == r, place * DRAFT + token_ids % DRAFT, rows)
    return rows


def gather_chips(buffer, send_sem, recv_sem, wide, me, chips, between=None):
    chip, core = me // 2, me % 2
    mate = chip * 2 + 1 - core
    sends = []

    def send(block, target, slot):
        copy = remote(
            buffer.at[block],
            buffer.at[block],
            send_sem.at[slot],
            recv_sem.at[block],
            wide,
            target,
        )
        copy.start()
        sends.append(copy)

    for off in range(1, chips):
        send(me, lax.rem(chip + off, chips) * 2 + core, off)
    send(me, mate, 0)
    if between is not None:
        between()

    def arrived(block):
        remote(
            buffer.at[block], buffer.at[block], send_sem.at[0], recv_sem.at[block], wide, mate
        ).wait_recv()

    for off in range(1, chips):
        block = lax.rem(chip - off + chips, chips) * 2 + core
        arrived(block)
        send(block, mate, chips - 1 + off)
    arrived(mate)
    for off in range(1, chips):
        arrived(lax.rem(chip - off + chips, chips) * 2 + 1 - core)
    for copy in sends:
        copy.wait_send()


def front_kernel(
    wide_count,
    narrow_count,
    owner_ref,
    hidden_hbm,
    mask_hbm,
    gain_hbm,
    query_gain_hbm,
    wkv_hbm,
    wq_hbm,
    q_out,
    mask_out,
    kv_out,
    hidden_ref,
    mask_ref,
    gain_ref,
    query_gain_ref,
    wkv_ref,
    wq,
    staged,
    landed,
    gathered,
    q_all,
    kv_part,
    kv_land,
    kv_pair,
    small_sem,
    wq_sem,
    a_send,
    a_recv,
    g_send,
    g_recv,
    q_send,
    q_recv,
    k_send,
    k_recv,
):
    wide, me = lax.axis_index("wide"), lax.axis_index("narrow")
    chips = narrow_count // 2
    chip, core = me // 2, me % 2
    mate = chip * 2 + 1 - core
    tokens, features = hidden_ref.shape
    requests = tokens // DRAFT
    part = tokens // wide_count
    per_head = HQ // narrow_count
    per_key = narrow_count // KVH

    small = [
        pltpu.make_async_copy(source, held, small_sem.at[i])
        for i, (source, held) in enumerate(
            [
                (hidden_hbm, hidden_ref),
                (mask_hbm, mask_ref),
                (gain_hbm, gain_ref),
                (query_gain_hbm, query_gain_ref),
                (wkv_hbm, wkv_ref),
            ]
        )
    ]
    load = pltpu.make_async_copy(wq_hbm, wq, wq_sem)
    for copy in small + [load]:
        copy.start()
    peers = [(lax.rem(wide + off, wide_count), me) for off in range(1, wide_count)]
    peers += [(wide, lax.rem(chip + off, chips) * 2 + core) for off in range(1, chips)]
    peers += [(wide, mate)]
    greet(peers)
    for copy in small[:2]:
        copy.wait()

    target = slot_rows(
        owner_ref, lax.broadcasted_iota(jnp.int32, (tokens, tokens), 1), part // DRAFT
    )
    chosen = lax.broadcasted_iota(jnp.int32, (tokens, tokens), 0) == target
    chosen = jnp.where(chosen, 1.0, 0.0).astype(jnp.bfloat16)
    staged[:, :features] = jnp.dot(
        chosen, hidden_ref[...], preferred_element_type=jnp.float32
    ).astype(jnp.bfloat16)
    staged[:, features:] = jnp.dot(
        chosen, mask_ref[...], preferred_element_type=jnp.float32
    ).astype(jnp.bfloat16)

    sends = []
    for off in range(1, wide_count):
        there = lax.rem(wide + off, wide_count)
        copy = remote(
            staged.at[pl.ds(pl.multiple_of(there * part, part), part)],
            landed.at[wide],
            a_send.at[off],
            a_recv.at[wide],
            there,
            me,
        )
        copy.start()
        sends.append(copy)
    landed[wide] = staged[pl.ds(pl.multiple_of(wide * part, part), part)]
    for off in range(1, wide_count):
        there = lax.rem(wide - off + wide_count, wide_count)
        remote(
            landed.at[there], landed.at[there], a_send.at[0], a_recv.at[there], there, me
        ).wait_recv()
    rows = landed[...].reshape(tokens, features + tokens)
    gathered[me] = rows[:, :features]
    mask_out[...] = rows[:, features:]
    gather_chips(gathered, g_send, g_recv, wide, me, chips)
    for copy in sends:
        copy.wait_send()

    for copy in small[2:]:
        copy.wait()
    squares = jnp.zeros((tokens, 1), jnp.float32)
    for j in range(narrow_count):
        block = gathered[j].astype(jnp.float32)
        squares += jnp.sum(block * block, axis=1, keepdims=True)
    factor = lax.rsqrt(squares * (1.0 / (narrow_count * features)) + epsilon)

    def normed(j):
        return (gathered[j].astype(jnp.float32) * factor * gain_ref[j]).astype(jnp.bfloat16)

    keyval = jnp.dot(normed(me), wkv_ref[...], preferred_element_type=jnp.float32)
    for c in range(chips):
        k = c * 2 // per_key
        kv_part[c, :, :HD] = keyval[:, k * HD : (k + 1) * HD]
        kv_part[c, :, HD:] = keyval[:, (KVH + k) * HD : (KVH + k + 1) * HD]
    load.wait()
    total = jnp.zeros((tokens, per_head * HD), jnp.float32)
    for j in range(narrow_count):
        total += jnp.dot(
            normed(j),
            wq[j * features : (j + 1) * features, :],
            preferred_element_type=jnp.float32,
        )
    for h in range(per_head):
        one = rms_norm(total[:, h * HD : (h + 1) * HD], query_gain_ref[...]).astype(jnp.bfloat16)
        q_all[me, :, h * DRAFT : (h + 1) * DRAFT, :] = one.reshape(requests, DRAFT, HD)

    kv_sends = []

    def send_kv():
        for off in range(1, chips):
            there = lax.rem(chip + off, chips)
            copy = remote(
                kv_part.at[there],
                kv_land.at[chip],
                k_send.at[off],
                k_recv.at[chip],
                wide,
                there * 2 + core,
            )
            copy.start()
            kv_sends.append(copy)

    gather_chips(q_all, q_send, q_recv, wide, me, chips, send_kv)
    summed = kv_part[chip]
    for off in range(1, chips):
        there = lax.rem(chip - off + chips, chips)
        remote(
            kv_land.at[there],
            kv_land.at[there],
            k_send.at[0],
            k_recv.at[there],
            wide,
            there * 2 + core,
        ).wait_recv()
        summed = summed + kv_land[there]
    kv_pair[0] = summed
    copy = remote(
        kv_pair.at[0], kv_pair.at[1], k_send.at[0], k_recv.at[chips], wide, mate
    )
    copy.start()
    kv_sends.append(copy)
    q_out[...] = q_all[...]
    remote(
        kv_pair.at[0], kv_pair.at[1], k_send.at[0], k_recv.at[chips], wide, mate
    ).wait_recv()
    kv_out[...] = kv_pair[0] + kv_pair[1]
    for copy in kv_sends:
        copy.wait_send()


def back_kernel(
    wide_count,
    narrow_count,
    owner_ref,
    lengths_ref,
    q_ref,
    mask_ref,
    kv_ref,
    key_gain_ref,
    k_hbm,
    v_hbm,
    wo_hbm,
    out_ref,
    wo,
    o_part,
    s_part,
    columns,
    o_land,
    s_land,
    att,
    mate_part,
    mate_land,
    chip_part,
    chip_land,
    y,
    y_land,
    wo_sem,
    o_send,
    o_recv,
    s_send,
    s_recv,
    m_send,
    m_recv,
    c_send,
    c_recv,
    y_send,
    y_recv,
):
    wide, me = lax.axis_index("wide"), lax.axis_index("narrow")
    chips = narrow_count // 2
    chip, core = me // 2, me % 2
    mate = chip * 2 + 1 - core
    _, requests, rows, _ = q_ref.shape
    tokens, features = out_ref.shape
    part = tokens // wide_count
    per_head = rows // DRAFT

    load = pltpu.make_async_copy(wo_hbm, wo, wo_sem)
    load.start()
    peers = [(lax.rem(wide + off, wide_count), me) for off in range(1, wide_count)]
    peers += [(wide, lax.rem(me + off, narrow_count)) for off in range(1, narrow_count)]
    greet(peers)

    sends = []
    span = k_hbm.shape[1]
    per_key = narrow_count // KVH
    my_key = me // per_key
    lanes = lax.broadcasted_iota(jnp.int32, (per_key * rows, HD), 1)
    ones = jnp.ones((span, HD), jnp.bfloat16)

    def send(there):
        for copy in (
            remote(
                s_part.at[there], s_land.at[me], s_send.at[there], s_recv.at[me], wide, there
            ),
            remote(
                o_part.at[there], o_land.at[me], o_send.at[there], o_recv.at[me], wide, there
            ),
        ):
            copy.start()
            sends.append(copy)

    for step in range(1, KVH + 1):
        key = lax.rem(my_key + step, KVH)
        first = key * per_key

        def body(k_ref, v_ref, first=first):
            for i in range(PAIR):
                r = pl.program_id(0) * PAIR + i
                q = jnp.concatenate([q_ref[first + d, r] for d in range(per_key)], axis=0)
                scores = lax.dot_general(
                    q, k_ref[i], (((1,), (1,)), ((), ())), preferred_element_type=jnp.float32
                )
                remaining = lengths_ref[r] - me * span
                live = lax.broadcasted_iota(jnp.int32, scores.shape, 1) < remaining
                scores = jnp.where(live, scores, masked_fill)
                top = jnp.max(scores, axis=1, keepdims=True) * SCALE
                weights = jnp.exp2(scores * SCALE - top).astype(jnp.bfloat16)
                both = jnp.dot(
                    weights,
                    jnp.concatenate([v_ref[i], ones], axis=1),
                    preferred_element_type=jnp.float32,
                )
                for d in range(per_key):
                    o_part[first + d, r] = both[d * rows : (d + 1) * rows, :HD].astype(
                        jnp.bfloat16
                    )
                held = jnp.where(lanes == r, top, columns[...])
                columns[...] = jnp.where(lanes == requests + r, both[:, HD:], held)

        columns[...] = jnp.zeros_like(columns)
        spec = pl.BlockSpec((PAIR, span, HD), lambda r, key=key: (r, 0, key))
        pltpu.emit_pipeline(body, grid=(requests // PAIR,), in_specs=[spec, spec])(k_hbm, v_hbm)
        turned = columns[...].T
        for d in range(per_key):
            for which in range(2):
                s_part[first + d, which] = turned[
                    which * requests : (which + 1) * requests, d * rows : (d + 1) * rows
                ]
        if step < KVH:
            for d in range(per_key):
                send(first + d)
        else:
            for off in range(1, per_key):
                send(first + lax.rem(me - first + off, per_key))
    s_land[me] = s_part[me]
    o_land[me] = o_part[me]

    draft_keys = rms_norm(kv_ref[:, :HD], key_gain_ref[...]).astype(jnp.bfloat16)
    draft_values = kv_ref[:, HD:].astype(jnp.bfloat16)
    request_of = lax.broadcasted_iota(jnp.int32, (rows, tokens), 1) // DRAFT
    drafts = []
    for r in range(requests):
        scores = (
            lax.dot_general(
                q_ref[me, r], draft_keys, (((1,), (1,)), ((), ())), preferred_element_type=jnp.float32
            )
            * SCALE
        )
        mask = mask_ref[r * DRAFT : (r + 1) * DRAFT, :].astype(jnp.float32)
        seen = (jnp.concatenate([mask] * per_head, axis=0) == 1.0) & (request_of == r)
        scores = jnp.where(seen, scores, masked_fill)
        top = jnp.max(scores, axis=1, keepdims=True)
        weights = jnp.where(seen, jnp.exp2(scores - top), 0.0)
        total = jnp.sum(weights, axis=1, keepdims=True)
        summed = jnp.dot(
            weights.astype(jnp.bfloat16), draft_values, preferred_element_type=jnp.float32
        )
        drafts.append((top, total, summed))

    for off in range(1, narrow_count):
        there = lax.rem(me - off + narrow_count, narrow_count)
        remote(
            s_land.at[there], s_land.at[there], s_send.at[0], s_recv.at[there], wide, there
        ).wait_recv()
        remote(
            o_land.at[there], o_land.at[there], o_send.at[0], o_recv.at[there], wide, there
        ).wait_recv()

    tops = s_land[0, 0]
    for j in range(1, narrow_count):
        tops = jnp.maximum(tops, s_land[j, 0])
    scaling = [jnp.exp2(s_land[j, 0] - tops) for j in range(narrow_count)]
    totals = scaling[0] * s_land[0, 1]
    for j in range(1, narrow_count):
        totals = totals + scaling[j] * s_land[j, 1]
    listed = jnp.concatenate(scaling + [tops, totals], axis=0)
    filled = -(-listed.shape[0] // 128) * 128
    if filled > listed.shape[0]:
        listed = jnp.concatenate(
            [listed, jnp.zeros((filled - listed.shape[0], rows), jnp.float32)], axis=0
        )
    turned = listed.T

    def column(which, r):
        place = which * requests + r
        return turned[:, place : place + 1]

    for r in range(requests):
        draft_top, draft_total, joined = drafts[r]
        cache_top = column(narrow_count, r)
        top = jnp.maximum(cache_top, draft_top)
        cache_scale, draft_scale = jnp.exp2(cache_top - top), jnp.exp2(draft_top - top)
        summed = column(0, r) * o_land[0, r].astype(jnp.float32)
        for j in range(1, narrow_count):
            summed = summed + column(j, r) * o_land[j, r].astype(jnp.float32)
        total = column(narrow_count + 1, r) * cache_scale + draft_total * draft_scale
        value = ((summed * cache_scale + joined * draft_scale) / total).astype(jnp.bfloat16)
        for h in range(per_head):
            att[r * DRAFT : (r + 1) * DRAFT, h * HD : (h + 1) * HD] = value[
                h * DRAFT : (h + 1) * DRAFT
            ]

    load.wait()

    def terms(device):
        place = pl.ds(pl.multiple_of(device * features, features), features)
        return jnp.dot(att[...], wo[:, place], preferred_element_type=jnp.float32)

    for step in range(1, chips + 1):
        there = lax.rem(chip + step, chips)
        mate_part[there] = terms(there * 2 + 1 - core).astype(jnp.bfloat16)
        copy = remote(
            mate_part.at[there],
            mate_land.at[there],
            m_send.at[there],
            m_recv.at[there],
            wide,
            mate,
        )
        copy.start()
        sends.append(copy)
    summed = None
    for step in range(1, chips + 1):
        there = lax.rem(chip + step, chips)
        value = terms(there * 2 + core)
        remote(
            mate_land.at[there], mate_land.at[there], m_send.at[0], m_recv.at[there], wide, mate
        ).wait_recv()
        value = value + mate_land[there].astype(jnp.float32)
        if step < chips:
            chip_part[there] = value.astype(jnp.bfloat16)
            copy = remote(
                chip_part.at[there],
                chip_land.at[chip],
                c_send.at[there],
                c_recv.at[chip],
                wide,
                there * 2 + core,
            )
            copy.start()
            sends.append(copy)
        else:
            summed = value
    for off in range(1, chips):
        there = lax.rem(chip - off + chips, chips)
        remote(
            chip_land.at[there],
            chip_land.at[there],
            c_send.at[0],
            c_recv.at[there],
            wide,
            there * 2 + core,
        ).wait_recv()
        summed = summed + chip_land[there].astype(jnp.float32)
    y[...] = summed.astype(jnp.bfloat16)

    for off in range(1, wide_count):
        there = lax.rem(wide + off, wide_count)
        copy = remote(
            y.at[pl.ds(pl.multiple_of(there * part, part), part)],
            y_land.at[wide],
            y_send.at[off],
            y_recv.at[wide],
            there,
            me,
        )
        copy.start()
        sends.append(copy)
    y_land[wide] = y[pl.ds(pl.multiple_of(wide * part, part), part)]
    source = slot_rows(
        owner_ref, lax.broadcasted_iota(jnp.int32, (tokens, tokens), 0), part // DRAFT
    )
    chosen = lax.broadcasted_iota(jnp.int32, (tokens, tokens), 1) == source
    chosen = jnp.where(chosen, 1.0, 0.0).astype(jnp.bfloat16)
    for off in range(1, wide_count):
        there = lax.rem(wide - off + wide_count, wide_count)
        remote(
            y_land.at[there], y_land.at[there], y_send.at[0], y_recv.at[there], there, me
        ).wait_recv()
    out_ref[...] = jnp.dot(
        chosen, y_land[...].reshape(tokens, features), preferred_element_type=jnp.float32
    ).astype(jnp.bfloat16)
    for copy in sends:
        copy.wait_send()


def local(
    hidden,
    norm_gain,
    w_query,
    w_keyval,
    query_gain,
    key_gain,
    cache_keys,
    cache_values,
    cache_lengths,
    owner_rank,
    draft_mask,
    w_output,
):
    narrow_count = lax.axis_size("narrow")
    wide_count = lax.axis_size("wide")
    tokens, features = hidden.shape
    requests = tokens // DRAFT
    per_head = HQ // narrow_count
    part = tokens // wide_count
    chips = narrow_count // 2
    rows = per_head * DRAFT
    vmem = pl.BlockSpec(memory_space=pltpu.VMEM)
    smem = pl.BlockSpec(memory_space=pltpu.SMEM)
    anywhere = pl.BlockSpec(memory_space=pl.ANY)
    dma = pltpu.SemaphoreType.DMA
    bf16, f32 = jnp.bfloat16, jnp.float32

    mask_rows = jnp.tile(draft_mask.reshape(tokens, DRAFT).astype(bf16), (1, tokens // DRAFT))
    all_queries, owned_mask, keyval = pl.pallas_call(
        functools.partial(front_kernel, wide_count, narrow_count),
        out_shape=[
            jax.ShapeDtypeStruct((narrow_count, requests, rows, HD), bf16),
            jax.ShapeDtypeStruct((tokens, tokens), bf16),
            jax.ShapeDtypeStruct((tokens, 2 * HD), f32),
        ],
        in_specs=[smem] + [anywhere] * 6,
        out_specs=[vmem] * 3,
        scratch_shapes=[
            pltpu.VMEM(hidden.shape, bf16),
            pltpu.VMEM((tokens, tokens), bf16),
            pltpu.VMEM((narrow_count, 1, features), f32),
            pltpu.VMEM((1, HD), f32),
            pltpu.VMEM(w_keyval.shape, bf16),
            pltpu.VMEM(w_query.shape, bf16),
            pltpu.VMEM((tokens, features + tokens), bf16),
            pltpu.VMEM((wide_count, part, features + tokens), bf16),
            pltpu.VMEM((narrow_count, tokens, features), bf16),
            pltpu.VMEM((narrow_count, requests, rows, HD), bf16),
            pltpu.VMEM((chips, tokens, 2 * HD), f32),
            pltpu.VMEM((chips, tokens, 2 * HD), f32),
            pltpu.VMEM((2, tokens, 2 * HD), f32),
            dma((5,)),
            dma,
            dma((wide_count,)),
            dma((wide_count,)),
            dma((narrow_count,)),
            dma((narrow_count,)),
            dma((narrow_count,)),
            dma((narrow_count,)),
            dma((chips,)),
            dma((chips + 1,)),
        ],
        compiler_params=pltpu.CompilerParams(
            collective_id=0, has_side_effects=True, vmem_limit_bytes=56 * MIB
        ),
    )(
        owner_rank,
        hidden,
        mask_rows,
        norm_gain.reshape(narrow_count, 1, features),
        query_gain.reshape(1, HD),
        w_keyval,
        w_query,
    )

    return pl.pallas_call(
        functools.partial(back_kernel, wide_count, narrow_count),
        out_shape=jax.ShapeDtypeStruct((tokens, features), bf16),
        in_specs=[smem, smem, vmem, vmem, vmem, vmem, anywhere, anywhere, anywhere],
        out_specs=vmem,
        scratch_shapes=[
            pltpu.VMEM(w_output.shape, bf16),
            pltpu.VMEM((narrow_count, requests, rows, HD), bf16),
            pltpu.VMEM((narrow_count, 2, requests, rows), f32),
            pltpu.VMEM((narrow_count // KVH * rows, HD), f32),
            pltpu.VMEM((narrow_count, requests, rows, HD), bf16),
            pltpu.VMEM((narrow_count, 2, requests, rows), f32),
            pltpu.VMEM((tokens, per_head * HD), bf16),
            pltpu.VMEM((chips, tokens, features), bf16),
            pltpu.VMEM((chips, tokens, features), bf16),
            pltpu.VMEM((chips, tokens, features), bf16),
            pltpu.VMEM((chips, tokens, features), bf16),
            pltpu.VMEM((tokens, features), bf16),
            pltpu.VMEM((wide_count, part, features), bf16),
            dma,
            dma((narrow_count,)),
            dma((narrow_count,)),
            dma((narrow_count,)),
            dma((narrow_count,)),
            dma((chips,)),
            dma((chips,)),
            dma((chips,)),
            dma((chips,)),
            dma((wide_count,)),
            dma((wide_count,)),
        ],
        compiler_params=pltpu.CompilerParams(
            collective_id=1, has_side_effects=True, vmem_limit_bytes=56 * MIB
        ),
    )(
        owner_rank,
        cache_lengths,
        all_queries,
        owned_mask,
        keyval,
        key_gain.reshape(1, HD),
        cache_keys,
        cache_values,
        w_output,
    )


def solution(mesh):
    in_specs = (
        P("wide", "narrow"),
        P(),
        P(None, "narrow"),
        P("narrow", None),
        P(),
        P(),
        P("wide", "narrow", None),
        P("wide", "narrow", None),
        P("wide"),
        P("wide"),
        P("wide", None, None),
        P("narrow", None),
    )
    out_specs = P("wide", "narrow")
    return jax.shard_map(local, mesh=mesh, in_specs=in_specs, out_specs=out_specs, check_vma=False)
```
